32 devices in a mesh: groups: 1, ep: 32 (over z, y, x, core).
Axes of the slice: x: 2, y: 2, z: 4, core: 2. Of those that a mesh axis runs over, the one named last changes fastest.
Arguments:
- moe_input: bfloat16 [1024, 3584], P(('groups', 'ep')), may hold values from -6 to 6
- route_ids: int32 [1024, 8], P(('groups', 'ep')), may hold values from 0 to 15, all different within a row; in each aligned block of 32 rows (0 to 31, 32 to 63, ...) at most 16 rows name the same one
- route_weights: float32 [1024, 8], P(('groups', 'ep')), may hold values from 0.05 to 1
- gate_weight: bfloat16 [32, 3584, 512], P('ep'), may hold values from -0.09375 to 0.09375
- up_weight: bfloat16 [32, 3584, 512], P('ep'), may hold values from -0.09375 to 0.09375
- down_weight: bfloat16 [32, 512, 3584], P('ep'), may hold values from -0.1875 to 0.1875
Outputs:
- moe_out: bfloat16 [1024, 3584], P(('groups', 'ep'))
The draws below stay inside these ranges and needn't reach their ends.
Inputs may be any that keep to these rules, and one draw needn't show every extreme that they name: `route_ids`: each row names 8 different experts; within the 32 rows of one device no expert is named by more than 16 rows.
All inputs are finite; a program needn't handle non-finite values.
Results may differ from the reference program's by a relative error of at most 0.0058.
Values may be sent and summed in bfloat16 or wider, within the bound.
No kernel may reach another device: no remote copies, remote signals or barrier semaphores. Data moves between devices by JAX's collectives and lax.ppermute only.
A program may use at most 64 MiB of HBM per device.

```python
import math
import jax
import jax.numpy as jnp
import numpy as np
from jax import lax

D = 3584
TOP = 8
FF_DEV = 512
ROWS_DEV = 32
FF = 1024
EXPERTS = 16
CAP = 16
ROWS = 1024
N_EP = 32


def levels(stream_key, extent, pieces, smallest, top_value):
    loudness, own = 1.0, jax.random.fold_in(stream_key, 6)
    for position, parts in pieces:
        heights = jnp.exp(jax.random.uniform(jax.random.fold_in(own, position), (parts,), jnp.float32, smallest / len(pieces), top_value / len(pieces)))
        loudness = loudness * jnp.repeat(heights, extent[position] // parts).reshape([-1 if axis == position else 1 for axis in range(len(extent))])
    return loudness


def shared_out(rng, own, number, rows, amount, top, most, slope):
    order = jax.random.permutation(rng, amount)
    packed, common = load_shares(amount, rows * top, most, slope, True), load_shares(amount, rows * top, most, slope, False)
    places = jnp.arange(amount)

    def named(lengths, offset_by):
        used = int((lengths > 0).sum())
        fixed = max(1, used // 4)
        moved = fixed + (places - fixed + offset_by * (used - fixed)) % max(1, amount - fixed)
        return jnp.zeros((amount,), jnp.int32).at[order[jnp.where(places < fixed, places, moved)]].set(jnp.asarray(lengths, jnp.int32))

    lengths = jnp.where(number % 4 == 0, named(packed, number // 4), named(common, number - number // 4 - 1))
    mixed = jax.random.permutation(jax.random.fold_in(own, 3), amount)
    donor, taker = mixed[0:amount // 2 * 2:2], mixed[1:amount // 2 * 2:2]
    room = jnp.minimum(lengths[donor] - 1, most - lengths[taker]) // 2
    room = jnp.where((donor == order[0]) | (taker == order[0]) | (lengths[taker] == 0), 0, jnp.maximum(room, 0))
    moved = jax.random.randint(jax.random.fold_in(own, 4), (amount // 2,), 0, 1 << 20) % (room + 1)
    lengths = lengths.at[donor].add(-moved).at[taker].add(moved)
    items = jnp.searchsorted(jnp.cumsum(lengths), jnp.arange(rows * top), side="right").astype(jnp.int32)
    listing = items.reshape(top, rows).T
    listing = listing[jax.random.permutation(jax.random.fold_in(own, 1), rows)]
    offset_by = jax.random.randint(jax.random.fold_in(own, 2), (rows, 1), 0, top)
    return jnp.take_along_axis(listing, (jnp.arange(top)[None, :] + offset_by) % top, axis=1)


def load_shares(count, total, bound, lean, full):
    weights = [(1 << 20) // math.isqrt(grade ** lean) + 1 for grade in range(1, count + 1)]
    largest = bound if full else min(bound, max(-(-total // count), total * weights[0] // sum(weights)))
    least = 1 if total - largest >= count - 1 else 0
    holding, spare = [largest] + [least] * (count - 1), total - largest - least * (count - 1)
    while spare > 0:
        free = [i for i in range(1, count) if holding[i] < largest] or [i for i in range(1, count) if holding[i] < bound]
        whole, left = sum([weights[i] for i in free]), spare
        for i in free:
            more = min(bound - holding[i], max(1, left * weights[i] // whole), spare)
            holding[i] = holding[i] + more
            spare = spare - more
    return np.array(holding)


def centred(rng, extent, spread, reach, shards=(), held_as=jnp.bfloat16):
    array = jax.random.normal(rng, extent, jnp.float32) * spread
    if len(shards) > 0:
        array = levels(rng, extent, shards, -0.22, 0.18) * array
    return jnp.clip(array, min=-reach, max=reach).astype(held_as)


def setup_inputs(seed: int = 0, part: int = 0) -> dict:
    key_of = jax.random.split(jax.random.key(seed), 7)
    own_keys = jax.random.split(jax.random.fold_in(key_of[6], part), 7)
    moe_input = centred(own_keys[0], (ROWS, D), 1.0, 6.0, ((0, 32),))
    route_ids_keys = jax.random.split(jax.random.fold_in(own_keys[1], 1), ROWS // ROWS_DEV)
    route_ids_turns = jax.random.permutation(jax.random.fold_in(own_keys[1], 3), ROWS // ROWS_DEV)
    route_ids = jax.vmap(lambda own, number: shared_out(jax.random.fold_in(own_keys[1], 2), own, number, ROWS_DEV, EXPERTS, TOP, CAP, 2))(route_ids_keys, route_ids_turns).reshape((ROWS, TOP))
    route_weights = jnp.clip(jnp.exp(math.log(1.0) - 2.9957323 * jax.random.uniform(own_keys[2], (ROWS, TOP), jnp.float32) ** levels(own_keys[2], (ROWS, TOP), ((0, 32),), -0.2, 0.2)), 0.05, 1.0)
    gate_weight = centred(key_of[3], (EXPERTS * 2, D, FF_DEV), D ** -0.5, 0.09375, ((0, 32),))
    up_weight = centred(key_of[4], (EXPERTS * 2, D, FF_DEV), D ** -0.5, 0.09375, ((0, 32),))
    down_weight = centred(key_of[5], (EXPERTS * 2, FF_DEV, D), FF ** -0.5, 0.1875, ((0, 32),))
    return dict(moe_input=moe_input, route_ids=route_ids, route_weights=route_weights, gate_weight=gate_weight, up_weight=up_weight, down_weight=down_weight)


def expert_part(inputs, gate_slice, up_slice, down_slice):
    gate_value = jnp.dot(inputs.astype(jnp.float32), gate_slice.astype(jnp.float32), precision=lax.Precision.HIGHEST)
    up_value = jnp.dot(inputs.astype(jnp.float32), up_slice.astype(jnp.float32), precision=lax.Precision.HIGHEST)
    hidden = (jax.nn.silu(gate_value) * up_value).astype(jnp.bfloat16)
    return jnp.dot(hidden.astype(jnp.float32), down_slice.astype(jnp.float32), precision=lax.Precision.HIGHEST)


def reference(moe_input, route_ids, route_weights, gate_weight, up_weight, down_weight):
    most_rows = N_EP * CAP

    def one_expert(expert, total):
        chosen = route_ids == expert
        present = jnp.any(chosen, axis=1)
        picked = jnp.nonzero(present, size=most_rows, fill_value=ROWS)[0].astype(jnp.int32)
        bounded = jnp.minimum(picked, ROWS - 1).astype(jnp.int32)
        inputs = moe_input[bounded]
        factor = jnp.sum(jnp.where(chosen, route_weights, 0.0), axis=1)[bounded]
        factor = jnp.where(picked < ROWS, factor, 0.0)
        first_half = expert_part(inputs, gate_weight[2 * expert], up_weight[2 * expert], down_weight[2 * expert])
        second_half = expert_part(inputs, gate_weight[2 * expert + 1], up_weight[2 * expert + 1], down_weight[2 * expert + 1])
        rounded = lax.optimization_barrier((first_half + second_half).astype(jnp.bfloat16))
        result = rounded.astype(jnp.float32)
        return total.at[picked].add(factor[:, None] * result, mode="drop")

    total = lax.fori_loop(0, EXPERTS, one_expert, jnp.zeros((ROWS, D), jnp.float32))
    return total.astype(jnp.bfloat16)
```

```python
import functools

import jax
import jax.numpy as jnp
from jax import lax
from jax.experimental import pallas as pl
from jax.experimental.pallas import tpu as pltpu
from jax.sharding import PartitionSpec as P

F32, BF16 = jnp.float32, jnp.bfloat16
LANES = 128
TILE = 512


def whole_specs(count):
    return [pl.BlockSpec(memory_space=pltpu.VMEM)] * count


def call(kernel, out_shapes, *operands, flops=0):
    moved = sum(o.size * o.dtype.itemsize for o in operands)
    moved += sum(o.size * o.dtype.itemsize for o in out_shapes)
    return pl.pallas_call(
        kernel,
        out_shape=out_shapes,
        in_specs=whole_specs(len(operands)),
        out_specs=whole_specs(len(out_shapes)),
        compiler_params=pltpu.CompilerParams(vmem_limit_bytes=32 << 20),
        cost_estimate=pl.CostEstimate(flops=flops, bytes_accessed=moved, transcendentals=0),
    )(*operands)


def tiles(width):
    return [(start, min(TILE, width - start)) for start in range(0, width, TILE)]


def split3(value):
    high = value.astype(BF16)
    rest = value - high.astype(F32)
    middle = rest.astype(BF16)
    low = (rest - middle.astype(F32)).astype(BF16)
    return high, middle, low


def tag_kernel(experts, x_ref, ids_ref, weights_ref, out_ref):
    rows, width = x_ref.shape
    tag_lanes = out_ref.shape[1] - width
    lane = lax.broadcasted_iota(jnp.int32, (rows, tag_lanes), 1)
    expert = lane % experts
    group = lane // experts
    flags = jnp.zeros((rows, tag_lanes), F32)
    weights = jnp.zeros((rows, tag_lanes), F32)
    for k in range(ids_ref.shape[1]):
        match = ids_ref[:, k : k + 1] == expert
        flags = jnp.where(match, 1.0, flags)
        weights = jnp.where(match, weights_ref[:, k : k + 1], weights)
    high, middle, low = split3(weights)
    tag = jnp.where(
        group == 0,
        flags,
        jnp.where(
            group == 1,
            high.astype(F32),
            jnp.where(group == 2, middle.astype(F32), jnp.where(group == 3, low.astype(F32), 0.0)),
        ),
    )
    out_ref[:, :width] = x_ref[...]
    out_ref[:, width:] = tag.astype(BF16)


def pick_kernel(experts, cap, blocks, planes, e_ref, *refs):
    x_refs, outs = refs[:blocks], refs[blocks : blocks + planes]
    high_ref, middle_ref, low_ref = refs[blocks + planes :]
    rows = x_refs[0].shape[0]
    width = outs[0].shape[1]
    total = blocks * rows
    slots = blocks * cap
    tag = jnp.concatenate([x[:, width:] for x in x_refs], axis=0)
    tag_lanes = tag.shape[1]
    row = lax.broadcasted_iota(jnp.int32, (total, total), 0)
    col = lax.broadcasted_iota(jnp.int32, (total, total), 1)
    before = ((row // rows == col // rows) & (col < row)).astype(F32).astype(BF16)
    rank = jnp.dot(before, tag, preferred_element_type=F32)
    tag = tag.astype(F32)
    lane = lax.broadcasted_iota(jnp.int32, (total, tag_lanes), 1)
    block = lax.broadcasted_iota(jnp.int32, (total, 1), 0) // rows
    slot = lax.broadcasted_iota(jnp.int32, (total, planes * slots), 1)
    picked = jnp.zeros((total, planes * slots), F32)
    weight = jnp.zeros((total, planes * slots), F32)
    for j in range(planes):
        e = e_ref[0, j]
        here = lane == e
        flag = jnp.sum(jnp.where(here, tag, 0.0), axis=1, keepdims=True)
        place = jnp.sum(jnp.where(here, rank, 0.0), axis=1, keepdims=True).astype(jnp.int32)
        parts = (lane % experts == e) & (lane // experts >= 1) & (lane // experts <= 3)
        factor = jnp.sum(jnp.where(parts, tag, 0.0), axis=1, keepdims=True)
        target = jnp.where(flag > 0.0, j * slots + block * cap + place, -1)
        hit = slot == target
        picked = jnp.where(hit, 1.0, picked)
        weight = jnp.where(hit, factor, weight)
    high_ref[...], middle_ref[...], low_ref[...] = split3(weight)
    picker = picked.T.astype(BF16)
    for start, size in tiles(width):
        columns = pl.ds(start, size)
        x = jnp.concatenate([x[:, columns] for x in x_refs], axis=0)
        out = jnp.dot(picker, x, preferred_element_type=F32).astype(BF16)
        for j in range(planes):
            outs[j][:, columns] = out[j * slots : (j + 1) * slots]


def combine_kernel(blocks, planes, *refs):
    ret_refs = refs[:planes]
    high_ref, middle_ref, low_ref = refs[planes : planes + 3]
    outs = refs[planes + 3 :]
    rows, width = outs[0].shape
    for start, size in tiles(width):
        columns = pl.ds(start, size)
        y = jnp.concatenate([r[:, columns] for r in ret_refs], axis=0)
        total = jnp.dot(low_ref[...], y, preferred_element_type=F32)
        total += jnp.dot(middle_ref[...], y, preferred_element_type=F32)
        total += jnp.dot(high_ref[...], y, preferred_element_type=F32)
        for k in range(blocks):
            outs[k][:, columns] = total[k * rows : (k + 1) * rows].astype(outs[k].dtype)


def body(moe_input, route_ids, route_weights, gate_weight, up_weight, down_weight):
    rows, width = moe_input.shape
    top = route_ids.shape[1]
    devices = lax.axis_size("ep")
    experts = devices // 2
    cap = max(4, 2 * rows * top // devices)
    planes = min(4, experts)
    blocks = experts // planes
    slots = blocks * cap

    me = lax.axis_index("ep")
    my_block, my_plane = me // (2 * planes), me // 2 % planes

    def swap(array, mask):
        return lax.ppermute(array, "ep", [(i, i ^ mask) for i in range(devices)])

    tag_lanes = pl.cdiv(4 * experts, LANES) * LANES
    tagged = call(
        functools.partial(tag_kernel, experts),
        [jax.ShapeDtypeStruct((rows, width + tag_lanes), BF16)],
        moe_input, route_ids, route_weights,
    )[0]
    column = [tagged] + [swap(tagged, k * 2 * planes) for k in range(1, blocks)]
    targets = (my_block * planes + (my_plane ^ jnp.arange(planes, dtype=jnp.int32))).reshape(1, planes)
    picked = pl.pallas_call(
        functools.partial(pick_kernel, experts, cap, blocks, planes),
        out_shape=[jax.ShapeDtypeStruct((slots, width), BF16)] * planes
        + [jax.ShapeDtypeStruct((blocks * rows, planes * slots), BF16)] * 3,
        in_specs=[pl.BlockSpec(memory_space=pltpu.SMEM)] + whole_specs(blocks),
        out_specs=whole_specs(planes + 3),
        compiler_params=pltpu.CompilerParams(vmem_limit_bytes=32 << 20),
        cost_estimate=pl.CostEstimate(
            flops=2 * planes * slots * blocks * rows * width, bytes_accessed=6 * slots * planes * width, transcendentals=0
        ),
    )(targets, *column)
    outgoing, factors = picked[:planes], picked[planes:]
    mine = jnp.concatenate([outgoing[0]] + [swap(outgoing[j], 2 * j) for j in range(1, planes)], axis=0)
    others = swap(mine, 1)

    def hidden_of(inputs):
        gate_value = jnp.dot(inputs, gate_weight[0], preferred_element_type=F32)
        up_value = jnp.dot(inputs, up_weight[0], preferred_element_type=F32)
        return (jax.nn.silu(gate_value) * up_value).astype(BF16)

    hidden_mine = hidden_of(mine)
    part_others = jnp.dot(hidden_of(others), down_weight[0], preferred_element_type=F32).astype(BF16)
    from_pair = swap(part_others, 1)
    part_mine = jnp.dot(hidden_mine, down_weight[0], preferred_element_type=F32)
    result = (part_mine + from_pair.astype(F32)).astype(BF16)
    pieces = [result[j * slots : (j + 1) * slots] for j in range(planes)]
    returned = [pieces[0]] + [swap(pieces[j], 2 * j) for j in range(1, planes)]
    sums = call(
        functools.partial(combine_kernel, blocks, planes),
        [jax.ShapeDtypeStruct((rows, width), F32 if k == 0 else BF16) for k in range(blocks)],
        *returned, *factors,
        flops=6 * planes * slots * blocks * rows * width,
    )
    total = sums[0]
    for k in range(1, blocks):
        total = total + swap(sums[k], k * 2 * planes).astype(F32)
    return total.astype(BF16)


def solution(mesh):
    return jax.shard_map(
        body,
        mesh=mesh,
        in_specs=(
            P(("groups", "ep"), None),
            P(("groups", "ep"), None),
            P(("groups", "ep"), None),
            P("ep", None, None),
            P("ep", None, None),
            P("ep", None, None),
        ),
        out_specs=P(("groups", "ep"), None),
        check_vma=False,
    )
```

```python
import functools

import jax
import jax.numpy as jnp
from jax import lax
from jax.experimental import pallas as pl
from jax.experimental.pallas import tpu as pltpu
from jax.sharding import PartitionSpec as P

F32, BF16 = jnp.float32, jnp.bfloat16
LANES = 128
SHARE = (2, 3)
TILE = 512
VMEM_LIMIT = 24 << 20


def call(kernel, out_shapes, *operands, flops=0, scalars=0):
    moved = sum(o.size * o.dtype.itemsize for o in operands)
    moved += sum(o.size * o.dtype.itemsize for o in out_shapes)
    vmem = pl.BlockSpec(memory_space=pltpu.VMEM)
    smem = pl.BlockSpec(memory_space=pltpu.SMEM)
    return pl.pallas_call(
        kernel,
        out_shape=out_shapes,
        in_specs=[smem] * scalars + [vmem] * (len(operands) - scalars),
        out_specs=[vmem] * len(out_shapes),
        compiler_params=pltpu.CompilerParams(vmem_limit_bytes=VMEM_LIMIT),
        cost_estimate=pl.CostEstimate(flops=flops, bytes_accessed=moved, transcendentals=0),
    )(*operands)


def shaped(count, shape, dtype=BF16):
    return [jax.ShapeDtypeStruct(shape, dtype) for _ in range(count)]


def tiles(width):
    return [(start, min(TILE, width - start)) for start in range(0, width, TILE)]


def split3(value):
    high = value.astype(BF16)
    rest = value - high.astype(F32)
    middle = rest.astype(BF16)
    low = (rest - middle.astype(F32)).astype(BF16)
    return high, middle, low


def tag_kernel(experts, x_ref, ids_ref, weights_ref, first_ref, second_ref):
    rows, width = x_ref.shape
    split = first_ref.shape[1] - (first_ref.shape[1] + second_ref.shape[1] - width) // 2
    tag_lanes = first_ref.shape[1] - split
    lane = lax.broadcasted_iota(jnp.int32, (rows, tag_lanes), 1)
    expert = lane % experts
    group = lane // experts
    flags = jnp.zeros((rows, tag_lanes), F32)
    weights = jnp.zeros((rows, tag_lanes), F32)
    for k in range(ids_ref.shape[1]):
        match = ids_ref[:, k : k + 1] == expert
        flags = jnp.where(match, 1.0, flags)
        weights = jnp.where(match, weights_ref[:, k : k + 1], weights)
    parts = [flags] + [part.astype(F32) for part in split3(weights)]
    tag = jnp.zeros((rows, tag_lanes), F32)
    for number, part in enumerate(parts):
        tag = jnp.where(group == number, part, tag)
    first_ref[:, :split] = x_ref[:, :split]
    first_ref[:, split:] = tag.astype(BF16)
    second_ref[:, : width - split] = x_ref[:, split:]
    second_ref[:, width - split :] = tag.astype(BF16)


def pick_kernel(experts, cap, sources, targets, e_ref, *refs):
    x_refs, outs = refs[:sources], refs[sources : sources + targets]
    high_ref, middle_ref, low_ref = refs[sources + targets :]
    rows = x_refs[0].shape[0]
    width = outs[0].shape[1]
    total = sources * rows
    slots = sources * cap
    tag = jnp.concatenate([x[:, width:] for x in x_refs], axis=0)
    tag_lanes = tag.shape[1]
    row = lax.broadcasted_iota(jnp.int32, (total, total), 0)
    col = lax.broadcasted_iota(jnp.int32, (total, total), 1)
    before = ((row // rows == col // rows) & (col < row)).astype(F32).astype(BF16)
    rank = jnp.dot(before, tag, preferred_element_type=F32)
    tag = tag.astype(F32)
    lane = lax.broadcasted_iota(jnp.int32, (total, tag_lanes), 1)
    source = lax.broadcasted_iota(jnp.int32, (total, 1), 0) // rows
    slot = lax.broadcasted_iota(jnp.int32, (total, targets * slots), 1)
    picked = jnp.zeros((total, targets * slots), F32)
    weight = jnp.zeros((total, targets * slots), F32)
    for t in range(targets):
        e = e_ref[0, t]
        here = lane == e
        flag = jnp.sum(jnp.where(here, tag, 0.0), axis=1, keepdims=True)
        place = jnp.sum(jnp.where(here, rank, 0.0), axis=1, keepdims=True).astype(jnp.int32)
        parts = (lane % experts == e) & (lane // experts >= 1) & (lane // experts <= 3)
        factor = jnp.sum(jnp.where(parts, tag, 0.0), axis=1, keepdims=True)
        hit = slot == jnp.where(flag > 0.0, t * slots + source * cap + place, -1)
        picked = jnp.where(hit, 1.0, picked)
        weight = jnp.where(hit, factor, weight)
    high_ref[...], middle_ref[...], low_ref[...] = split3(weight)
    picker = picked.T.astype(BF16)
    for start, size in tiles(width):
        columns = pl.ds(start, size)
        x = jnp.concatenate([x[:, columns] for x in x_refs], axis=0)
        out = jnp.dot(picker, x, preferred_element_type=F32).astype(BF16)
        for t in range(targets):
            outs[t][:, columns] = out[t * slots : (t + 1) * slots]


def combine_kernel(sources, targets, *refs):
    returned = refs[:targets]
    high_ref, middle_ref, low_ref = refs[targets : targets + 3]
    outs = refs[targets + 3 :]
    rows, width = outs[0].shape
    for start, size in tiles(width):
        columns = pl.ds(start, size)
        y = jnp.concatenate([r[:, columns] for r in returned], axis=0)
        total = jnp.dot(low_ref[...], y, preferred_element_type=F32)
        total += jnp.dot(middle_ref[...], y, preferred_element_type=F32)
        total += jnp.dot(high_ref[...], y, preferred_element_type=F32)
        for s in range(sources):
            outs[s][:, columns] = total[s * rows : (s + 1) * rows].astype(outs[s].dtype)


def reorder(blocks, planes, cap, inverse=False):
    count = blocks * planes * cap
    row = lax.broadcasted_iota(jnp.int32, (count, count), 1 if inverse else 0)
    col = lax.broadcasted_iota(jnp.int32, (count, count), 0 if inverse else 1)
    plane, block, place = row // (blocks * cap), row // cap % blocks, row % cap
    return (col == (block * planes + plane) * cap + place).astype(F32).astype(BF16)


def hidden_kernel(blocks, planes, cap, *refs):
    firsts, seconds = refs[:planes], refs[planes : planes + blocks]
    gate_ref, up_ref, hidden_ref = refs[planes + blocks :]
    split = firsts[0].shape[1]
    first = jnp.concatenate([r[...] for r in firsts], axis=0)
    second = jnp.concatenate([r[...] for r in seconds], axis=0)
    second = jnp.dot(reorder(blocks, planes, cap), second, preferred_element_type=F32).astype(BF16)

    def product(ref, columns):
        value = jnp.dot(first, ref[0, :split, columns], preferred_element_type=F32)
        return value + jnp.dot(second, ref[0, split:, columns], preferred_element_type=F32)

    for start in range(0, hidden_ref.shape[1], 256):
        columns = pl.ds(start, 256)
        gate_value = product(gate_ref, columns)
        up_value = product(up_ref, columns)
        hidden_ref[:, columns] = (gate_value * jax.nn.sigmoid(gate_value) * up_value).astype(BF16)


def down_kernel(blocks, planes, cap, hidden_ref, down_ref, first_ref, second_ref):
    split = first_ref.shape[1]
    hidden = hidden_ref[...]
    for start, size in tiles(split):
        part = jnp.dot(hidden, down_ref[0, :, pl.ds(start, size)], preferred_element_type=F32)
        first_ref[:, pl.ds(start, size)] = part.astype(BF16)
    hidden = jnp.dot(reorder(blocks, planes, cap, True), hidden, preferred_element_type=F32).astype(BF16)
    for start, size in tiles(second_ref.shape[1]):
        part = jnp.dot(hidden, down_ref[0, :, pl.ds(split + start, size)], preferred_element_type=F32)
        second_ref[:, pl.ds(start, size)] = part.astype(BF16)


def add_down_kernel(blocks, planes, cap, hidden_ref, down_ref, first_ref, second_ref, *outs):
    split = first_ref.shape[1]
    hidden = hidden_ref[...]

    def halves(hidden, base, other_ref, outs):
        rows = outs[0].shape[0]
        for start, size in tiles(other_ref.shape[1]):
            columns = pl.ds(start, size)
            part = jnp.dot(hidden, down_ref[0, :, pl.ds(base + start, size)], preferred_element_type=F32)
            both = (part + other_ref[:, columns].astype(F32)).astype(BF16)
            for number, out in enumerate(outs):
                out[:, columns] = both[number * rows : (number + 1) * rows]

    halves(hidden, 0, first_ref, outs[:planes])
    hidden = jnp.dot(reorder(blocks, planes, cap, True), hidden, preferred_element_type=F32).astype(BF16)
    halves(hidden, split, second_ref, outs[planes:])


def body(moe_input, route_ids, route_weights, gate_weight, up_weight, down_weight):
    rows, width = moe_input.shape
    top = route_ids.shape[1]
    devices = lax.axis_size("ep")
    experts = devices // 2
    cap = max(4, 2 * rows * top // devices)
    planes = min(4, experts)
    blocks = experts // planes
    slots = blocks * planes * cap
    split = width * SHARE[0] // (SHARE[1] * LANES) * LANES
    rest = width - split

    me = lax.axis_index("ep")
    my_block, my_plane = me // (2 * planes), me // 2 % planes

    def swap(array, mask):
        return lax.ppermute(array, "ep", [(i, i ^ mask) for i in range(devices)])

    def over_blocks(arrays):
        return [arrays[0]] + [swap(arrays[k], 2 * planes * k) for k in range(1, blocks)]

    def over_planes(arrays):
        return [arrays[0]] + [swap(arrays[j], 2 * j) for j in range(1, planes)]

    tag_lanes = pl.cdiv(4 * experts, LANES) * LANES
    tagged_first, tagged_second = call(
        functools.partial(tag_kernel, experts),
        shaped(1, (rows, split + tag_lanes)) + shaped(1, (rows, rest + tag_lanes)),
        moe_input, route_ids, route_weights,
    )
    plane_ids = my_block * planes + (my_plane ^ jnp.arange(planes, dtype=jnp.int32))
    block_ids = (my_block ^ jnp.arange(blocks, dtype=jnp.int32)) * planes + my_plane
    column = over_blocks([tagged_first] * blocks)
    plane = over_planes([tagged_second] * planes)

    def pick(arrays, targets, ids, columns):
        sources = len(arrays)
        out = call(
            functools.partial(pick_kernel, experts, cap, sources, targets),
            shaped(targets, (sources * cap, columns)) + shaped(3, (sources * rows, slots)),
            ids.reshape(1, targets), *arrays,
            flops=2 * slots * sources * rows * columns, scalars=1,
        )
        return out[:targets], out[targets:]

    first, first_factors = pick(column, planes, plane_ids, split)
    second, second_factors = pick(plane, blocks, block_ids, rest)
    first = over_planes(first)
    second = over_blocks(second)
    first_other = [swap(piece, 1) for piece in first]
    second_other = [swap(piece, 1) for piece in second]

    sizes = (blocks, planes, cap)
    hidden_width = gate_weight.shape[2]

    def hidden_of(first, second):
        return call(
            functools.partial(hidden_kernel, *sizes),
            shaped(1, (slots, hidden_width)),
            *first, *second, gate_weight, up_weight,
            flops=4 * slots * width * hidden_width,
        )[0]

    hidden_mine = hidden_of(first, second)
    hidden_other = hidden_of(first_other, second_other)
    parts = call(
        functools.partial(down_kernel, *sizes),
        shaped(1, (slots, split)) + shaped(1, (slots, rest)),
        hidden_other, down_weight,
        flops=2 * slots * width * hidden_width,
    )
    results = call(
        functools.partial(add_down_kernel, *sizes),
        shaped(planes, (blocks * cap, split)) + shaped(blocks, (planes * cap, rest)),
        hidden_mine, down_weight, swap(parts[0], 1), swap(parts[1], 1),
        flops=2 * slots * width * hidden_width,
    )
    first = over_planes(results[:planes])
    second = over_blocks(results[planes:])

    def combine(arrays, factors, sources, columns):
        return call(
            functools.partial(combine_kernel, sources, len(arrays)),
            shaped(1, (rows, columns), F32) + shaped(sources - 1, (rows, columns)),
            *arrays, *factors,
            flops=6 * slots * sources * rows * columns,
        )

    first = over_blocks(combine(first, first_factors, blocks, split))
    second = over_planes(combine(second, second_factors, planes, rest))

    def total(arrays):
        result = arrays[0]
        for array in arrays[1:]:
            result = result + array.astype(F32)
        return result.astype(BF16)

    return jnp.concatenate([total(first), total(second)], axis=1)


def solution(mesh):
    return jax.shard_map(
        body,
        mesh=mesh,
        in_specs=(
            P(("groups", "ep"), None),
            P(("groups", "ep"), None),
            P(("groups", "ep"), None),
            P("ep", None, None),
            P("ep", None, None),
            P("ep", None, None),
        ),
        out_specs=P(("groups", "ep"), None),
        check_vma=False,
    )
```

```python
import functools

import jax
import jax.numpy as jnp
from jax import lax
from jax.experimental import pallas as pl
from jax.experimental.pallas import tpu as pltpu
from jax.sharding import PartitionSpec as P

F32, BF16 = jnp.float32, jnp.bfloat16
LANES = 128
SHARE = (2, 3)
TILE = 512
CHUNK = 768
VMEM_LIMIT = 24 << 20
LOAD_LIMIT = 41 << 20
HEAD_LIMIT = 60 << 20
GROUPS = 1


def call(kernel, out_shapes, *operands, flops=0, scalars=0):
    moved = sum(o.size * o.dtype.itemsize for o in operands)
    moved += sum(o.size * o.dtype.itemsize for o in out_shapes)
    vmem = pl.BlockSpec(memory_space=pltpu.VMEM)
    smem = pl.BlockSpec(memory_space=pltpu.SMEM)
    return pl.pallas_call(
        kernel,
        out_shape=out_shapes,
        in_specs=[smem] * scalars + [vmem] * (len(operands) - scalars),
        out_specs=[vmem] * len(out_shapes),
        compiler_params=pltpu.CompilerParams(vmem_limit_bytes=VMEM_LIMIT),
        cost_estimate=pl.CostEstimate(flops=flops, bytes_accessed=moved, transcendentals=0),
    )(*operands)


def shaped(count, shape, dtype=BF16):
    return [jax.ShapeDtypeStruct(shape, dtype) for _ in range(count)]


def tiles(width):
    return [(start, min(TILE, width - start)) for start in range(0, width, TILE)]


def split3(value):
    high = value.astype(BF16)
    rest = value - high.astype(F32)
    middle = rest.astype(BF16)
    low = (rest - middle.astype(F32)).astype(BF16)
    return high, middle, low


def tag_kernel(experts, x_hbm, ids_hbm, weights_hbm, first_ref, second_ref, ids_in, weights_in, ids_ref, weights_ref, sems):
    rows, width = x_hbm.shape
    top = ids_hbm.shape[0]
    tag_lanes = (first_ref.shape[1] + second_ref.shape[1] - width) // 2
    split = first_ref.shape[1] - tag_lanes
    ids_ref[...] = jnp.full(ids_ref.shape, -1, jnp.int32)
    weights_ref[...] = jnp.zeros(weights_ref.shape, F32)
    small = [
        pltpu.make_async_copy(ids_hbm, ids_in, sems.at[0]),
        pltpu.make_async_copy(weights_hbm, weights_in, sems.at[1]),
    ]
    large = [
        pltpu.make_async_copy(x_hbm.at[:, :split], first_ref.at[:, :split], sems.at[2]),
        pltpu.make_async_copy(x_hbm.at[:, split:], second_ref.at[:, : width - split], sems.at[3]),
    ]
    for copy in small + large:
        copy.start()
    for copy in small:
        copy.wait()
    ids_ref[:, :rows] = ids_in[...]
    weights_ref[:, :rows] = weights_in[...]
    lanes = ids_ref.shape[1]
    row = lax.broadcasted_iota(jnp.int32, (tag_lanes, lanes), 0)
    expert = row % experts
    group = row // experts
    flags = jnp.zeros((tag_lanes, lanes), F32)
    weights = jnp.zeros((tag_lanes, lanes), F32)
    for k in range(top):
        match = ids_ref[k : k + 1, :] == expert
        flags = jnp.where(match, 1.0, flags)
        weights = jnp.where(match, weights_ref[k : k + 1, :], weights)
    parts = [flags] + [part.astype(F32) for part in split3(weights)]
    tag = jnp.zeros((tag_lanes, lanes), F32)
    for number, part in enumerate(parts):
        tag = jnp.where(group == number, part, tag)
    tag = tag.T[:rows].astype(BF16)
    first_ref[:, split:] = tag
    second_ref[:, width - split :] = tag
    for copy in large:
        copy.wait()


def tagged_parts(experts, split, moe_input, route_ids, route_weights):
    rows, width = moe_input.shape
    top = route_ids.shape[1]
    tag_lanes = pl.cdiv(4 * experts, LANES) * LANES
    lanes = pl.cdiv(rows, LANES) * LANES
    return pl.pallas_call(
        functools.partial(tag_kernel, experts),
        out_shape=shaped(1, (rows, split + tag_lanes)) + shaped(1, (rows, width - split + tag_lanes)),
        in_specs=[pl.BlockSpec(memory_space=pl.ANY)] * 3,
        out_specs=[pl.BlockSpec(memory_space=pltpu.VMEM)] * 2,
        scratch_shapes=[
            pltpu.VMEM((top, rows), jnp.int32),
            pltpu.VMEM((top, rows), F32),
            pltpu.VMEM((top, lanes), jnp.int32),
            pltpu.VMEM((top, lanes), F32),
            pltpu.SemaphoreType.DMA((4,)),
        ],
        compiler_params=pltpu.CompilerParams(vmem_limit_bytes=HEAD_LIMIT),
        cost_estimate=pl.CostEstimate(flops=0, bytes_accessed=4 * rows * width, transcendentals=0),
    )(moe_input, route_ids.T, route_weights.T)


def pick_kernel(experts, cap, sources, targets, e_ref, *refs):
    x_refs, outs = refs[:sources], refs[sources : sources + targets]
    high_ref, middle_ref, low_ref = refs[sources + targets :]
    rows = x_refs[0].shape[0]
    width = outs[0].shape[1]
    total = sources * rows
    slots = sources * cap
    tag = jnp.concatenate([x[:, width:] for x in x_refs], axis=0)
    tag_lanes = tag.shape[1]
    row = lax.broadcasted_iota(jnp.int32, (total, total), 0)
    col = lax.broadcasted_iota(jnp.int32, (total, total), 1)
    before = ((row // rows == col // rows) & (col < row)).astype(F32).astype(BF16)
    rank = jnp.dot(before, tag, preferred_element_type=F32)
    tag = tag.astype(F32)
    lane = lax.broadcasted_iota(jnp.int32, (total, tag_lanes), 1)
    source = lax.broadcasted_iota(jnp.int32, (total, 1), 0) // rows
    slot = lax.broadcasted_iota(jnp.int32, (total, targets * slots), 1)
    picked = jnp.zeros((total, targets * slots), F32)
    weight = jnp.zeros((total, targets * slots), F32)
    for t in range(targets):
        e = e_ref[0, t]
        here = lane == e
        flag = jnp.sum(jnp.where(here, tag, 0.0), axis=1, keepdims=True)
        place = jnp.sum(jnp.where(here, rank, 0.0), axis=1, keepdims=True).astype(jnp.int32)
        parts = (lane % experts == e) & (lane // experts >= 1) & (lane // experts <= 3)
        factor = jnp.sum(jnp.where(parts, tag, 0.0), axis=1, keepdims=True)
        hit = slot == jnp.where(flag > 0.0, t * slots + source * cap + place, -1)
        picked = jnp.where(hit, 1.0, picked)
        weight = jnp.where(hit, factor, weight)
    high_ref[...], middle_ref[...], low_ref[...] = split3(weight)
    picker = picked.T.astype(BF16)
    for start, size in tiles(width):
        columns = pl.ds(start, size)
        x = jnp.concatenate([x[:, columns] for x in x_refs], axis=0)
        out = jnp.dot(picker, x, preferred_element_type=F32).astype(BF16)
        for t in range(targets):
            outs[t][:, columns] = out[t * slots : (t + 1) * slots]


def combine_kernel(sources, targets, *refs):
    returned = refs[:targets]
    high_ref, middle_ref, low_ref = refs[targets : targets + 3]
    outs = refs[targets + 3 :]
    rows, width = outs[0].shape
    for start, size in tiles(width):
        columns = pl.ds(start, size)
        y = jnp.concatenate([r[:, columns] for r in returned], axis=0)
        total = jnp.dot(low_ref[...], y, preferred_element_type=F32)
        total += jnp.dot(middle_ref[...], y, preferred_element_type=F32)
        total += jnp.dot(high_ref[...], y, preferred_element_type=F32)
        for s in range(sources):
            outs[s][:, columns] = total[s * rows : (s + 1) * rows].astype(outs[s].dtype)


def final_kernel(*refs):
    terms, out_ref = refs[:-1], refs[-1]
    start = 0
    while terms:
        size = terms[0].shape[1]
        count = sum(r.shape[1] == size for r in terms)
        total = terms[0][...]
        for r in terms[1:count]:
            total = total + r[...].astype(F32)
        out_ref[:, pl.ds(start, size)] = total.astype(BF16)
        terms, start = terms[count:], start + size


def reorder(blocks, planes, cap, inverse=False):
    count = blocks * planes * cap
    row = lax.broadcasted_iota(jnp.int32, (count, count), 1 if inverse else 0)
    col = lax.broadcasted_iota(jnp.int32, (count, count), 0 if inverse else 1)
    plane, block, place = row // (blocks * cap), row // cap % blocks, row % cap
    return (col == (block * planes + plane) * cap + place).astype(F32).astype(BF16)


def hidden_kernel(blocks, planes, cap, *refs):
    firsts, seconds = refs[: planes * GROUPS], refs[planes * GROUPS : planes * GROUPS + blocks]
    gate_ref, up_ref, hidden_ref = refs[planes * GROUPS + blocks :]
    split = firsts[0].shape[1]
    first = jnp.concatenate([r[...] for r in firsts], axis=0)
    second = jnp.concatenate([r[...] for r in seconds], axis=0)
    second = jnp.dot(reorder(blocks, planes, cap), second, preferred_element_type=F32).astype(BF16)

    def product(ref, columns):
        value = jnp.dot(first, ref[0, :split, columns], preferred_element_type=F32)
        return value + jnp.dot(second, ref[0, split:, columns], preferred_element_type=F32)

    for start in range(0, hidden_ref.shape[1], 256):
        columns = pl.ds(start, 256)
        gate_value = product(gate_ref, columns)
        up_value = product(up_ref, columns)
        hidden_ref[:, columns] = (gate_value * jax.nn.sigmoid(gate_value) * up_value).astype(BF16)


def chunks(split, width):
    cuts = list(range(0, split, CHUNK)) + list(range(split, width, CHUNK)) + [width]
    return [(start, stop - start) for start, stop in zip(cuts[:-1], cuts[1:])]


def load_hidden_kernel(blocks, planes, cap, *refs):
    firsts, seconds = refs[: planes * GROUPS], refs[planes * GROUPS : planes * GROUPS + blocks]
    gate_hbm, up_hbm, down_hbm, hidden_ref, gate_ref, up_ref, down_ref, gate_sum, up_sum, sems = refs[planes * GROUPS + blocks :]
    split = firsts[0].shape[1]
    pieces = chunks(split, gate_ref.shape[1])
    copies = []
    for number, (start, size) in enumerate(pieces):
        depth = pl.ds(start, size)
        copies.append((
            pltpu.make_async_copy(gate_hbm.at[:, depth], gate_ref.at[:, depth], sems.at[0, number]),
            pltpu.make_async_copy(up_hbm.at[:, depth], up_ref.at[:, depth], sems.at[1, number]),
        ))
    last = pltpu.make_async_copy(down_hbm, down_ref, sems.at[0, len(pieces)])
    for pair in copies:
        pair[0].start()
        pair[1].start()
    last.start()
    first = jnp.concatenate([r[...] for r in firsts], axis=0)
    second = jnp.concatenate([r[...] for r in seconds], axis=0)
    second = jnp.dot(reorder(blocks, planes, cap), second, preferred_element_type=F32).astype(BF16)
    for number, (start, size) in enumerate(pieces):
        x = first[:, start : start + size] if start < split else second[:, start - split : start - split + size]
        depth = pl.ds(start, size)
        for copy, ref, total in zip(copies[number], (gate_ref, up_ref), (gate_sum, up_sum)):
            copy.wait()
            part = jnp.dot(x, ref[0, depth, :], preferred_element_type=F32)
            if number == 0:
                total[...] = part
            else:
                total[...] += part
    gate_value = gate_sum[...]
    hidden_ref[...] = (gate_value * jax.nn.sigmoid(gate_value) * up_sum[...]).astype(BF16)
    last.wait()


def load_hidden(sizes, first, second, *weights):
    slots = sizes[0] * sizes[1] * sizes[2]
    split = first[0].shape[1]
    width, hidden_width = weights[0].shape[1:]
    vmem = pl.BlockSpec(memory_space=pltpu.VMEM)
    return pl.pallas_call(
        functools.partial(load_hidden_kernel, *sizes),
        out_shape=shaped(1, (slots, hidden_width)) + [jax.ShapeDtypeStruct(w.shape, w.dtype) for w in weights],
        in_specs=[vmem] * (len(first) + len(second)) + [pl.BlockSpec(memory_space=pl.ANY)] * 3,
        out_specs=[vmem] * 4,
        scratch_shapes=[
            pltpu.VMEM((slots, hidden_width), F32),
            pltpu.VMEM((slots, hidden_width), F32),
            pltpu.SemaphoreType.DMA((2, len(chunks(split, width)) + 1)),
        ],
        compiler_params=pltpu.CompilerParams(vmem_limit_bytes=LOAD_LIMIT),
        cost_estimate=pl.CostEstimate(
            flops=4 * slots * width * hidden_width,
            bytes_accessed=sum(w.size * w.dtype.itemsize for w in weights),
            transcendentals=0,
        ),
    )(*first, *second, *weights)


def down_kernel(blocks, planes, cap, hidden_ref, down_ref, first_ref, second_ref):
    split = first_ref.shape[1]
    hidden = hidden_ref[...]
    for start, size in tiles(split):
        part = jnp.dot(hidden, down_ref[0, :, pl.ds(start, size)], preferred_element_type=F32)
        first_ref[:, pl.ds(start, size)] = part.astype(BF16)
    hidden = jnp.dot(reorder(blocks, planes, cap, True), hidden, preferred_element_type=F32).astype(BF16)
    for start, size in tiles(second_ref.shape[1]):
        part = jnp.dot(hidden, down_ref[0, :, pl.ds(split + start, size)], preferred_element_type=F32)
        second_ref[:, pl.ds(start, size)] = part.astype(BF16)


def add_down_kernel(blocks, planes, cap, hidden_ref, down_ref, first_ref, second_ref, *outs):
    split = first_ref.shape[1]
    hidden = hidden_ref[...]

    def halves(hidden, base, other_ref, outs):
        rows = outs[0].shape[0]
        for start, size in tiles(other_ref.shape[1]):
            columns = pl.ds(start, size)
            part = jnp.dot(hidden, down_ref[0, :, pl.ds(base + start, size)], preferred_element_type=F32)
            both = (part + other_ref[:, columns].astype(F32)).astype(BF16)
            for number, out in enumerate(outs):
                out[:, columns] = both[number * rows : (number + 1) * rows]

    halves(hidden, 0, first_ref, outs[: planes * GROUPS])
    hidden = jnp.dot(reorder(blocks, planes, cap, True), hidden, preferred_element_type=F32).astype(BF16)
    halves(hidden, split, second_ref, outs[planes * GROUPS :])


def body(moe_input, route_ids, route_weights, gate_weight, up_weight, down_weight):
    rows, width = moe_input.shape
    top = route_ids.shape[1]
    devices = lax.axis_size("ep")
    experts = devices // 2
    cap = max(4, 2 * rows * top // devices)
    planes = min(4, experts)
    blocks = experts // planes
    slots = blocks * planes * cap
    split = width * SHARE[0] // (SHARE[1] * LANES) * LANES
    rest = width - split

    me = lax.axis_index("ep")
    my_block, my_plane = me // (2 * planes), me // 2 % planes

    def swap(array, mask):
        return lax.ppermute(array, "ep", [(i, i ^ mask) for i in range(devices)])

    def over_blocks(arrays):
        return [arrays[0]] + [swap(arrays[k], 2 * planes * k) for k in range(1, blocks)]

    def over_planes(arrays):
        return [arrays[0]] + [swap(arrays[j], 2 * j) for j in range(1, planes)]

    tagged_first, tagged_second = tagged_parts(experts, split, moe_input, route_ids, route_weights)
    plane_ids = my_block * planes + (my_plane ^ jnp.arange(planes, dtype=jnp.int32))
    block_ids = (my_block ^ jnp.arange(blocks, dtype=jnp.int32)) * planes + my_plane
    column = over_blocks([tagged_first] * blocks)
    plane = over_planes([tagged_second] * planes)
    group = blocks // GROUPS

    def pick(arrays, targets, ids, columns):
        sources = len(arrays)
        out = call(
            functools.partial(pick_kernel, experts, cap, sources, targets),
            shaped(targets, (sources * cap, columns)) + shaped(3, (sources * rows, targets * sources * cap)),
            ids.reshape(1, targets), *arrays,
            flops=2 * targets * sources * cap * sources * rows * columns, scalars=1,
        )
        return out[:targets], out[targets:]

    first, first_factors = [], []
    for g in range(GROUPS):
        pieces, factors = pick(column[g * group : (g + 1) * group], planes, plane_ids, split)
        first.append(over_planes(pieces))
        first_factors.append(factors)
    second, second_factors = pick(plane, blocks, block_ids, rest)
    second = over_blocks(second)
    first = [first[g][j] for j in range(planes) for g in range(GROUPS)]
    first_other = [swap(piece, 1) for piece in first]
    second_other = [swap(piece, 1) for piece in second]

    sizes = (blocks, planes, cap)
    hidden_width = gate_weight.shape[2]

    def hidden_of(first, second):
        return call(
            functools.partial(hidden_kernel, *sizes),
            shaped(1, (slots, hidden_width)),
            *first, *second, gate_weight, up_weight,
            flops=4 * slots * width * hidden_width,
        )[0]

    hidden_other, gate_weight, up_weight, down_weight = load_hidden(
        sizes, first_other, second_other, gate_weight, up_weight, down_weight
    )
    hidden_mine = hidden_of(first, second)
    parts = call(
        functools.partial(down_kernel, *sizes),
        shaped(1, (slots, split)) + shaped(1, (slots, rest)),
        hidden_other, down_weight,
        flops=2 * slots * width * hidden_width,
    )
    results = call(
        functools.partial(add_down_kernel, *sizes),
        shaped(planes * GROUPS, (group * cap, split)) + shaped(blocks, (planes * cap, rest)),
        hidden_mine, down_weight, swap(parts[0], 1), swap(parts[1], 1),
        flops=2 * slots * width * hidden_width,
    )
    def combine(arrays, factors, sources, columns, own):
        return call(
            functools.partial(combine_kernel, sources, len(arrays)),
            shaped(own, (rows, columns), F32) + shaped(sources - own, (rows, columns)),
            *arrays, *factors,
            flops=6 * arrays[0].shape[0] * len(arrays) * sources * rows * columns,
        )

    first = []
    for g in reversed(range(GROUPS)):
        returned = over_planes(results[g : planes * GROUPS : GROUPS])
        first = list(combine(returned, first_factors[g], group, split, int(g == 0))) + first
    first = over_blocks(first)
    second = over_blocks(results[planes * GROUPS :])
    second = over_planes(combine(second, second_factors, planes, rest, 1))
    return call(final_kernel, shaped(1, (rows, width)), *first, *second)[0]


def solution(mesh):
    return jax.shard_map(
        body,
        mesh=mesh,
        in_specs=(
            P(("groups", "ep"), None),
            P(("groups", "ep"), None),
            P(("groups", "ep"), None),
            P("ep", None, None),
            P("ep", None, None),
            P("ep", None, None),
        ),
        out_specs=P(("groups", "ep"), None),
        check_vma=False,
    )
```

```python
import functools

import jax
import jax.numpy as jnp
from jax import lax
from jax.experimental import pallas as pl
from jax.experimental.pallas import tpu as pltpu
from jax.sharding import PartitionSpec as P

F32, BF16 = jnp.float32, jnp.bfloat16
LANES = 128
SHARE = (2, 3)
TILE = 512
CHUNK = 768
VMEM_LIMIT = 24 << 20
LOAD_LIMIT = 41 << 20
HEAD_LIMIT = 54 << 20
GROUPS = 1


def call(kernel, out_shapes, *operands, flops=0, scalars=0, scale=1.0):
    moved = sum(o.size * o.dtype.itemsize for o in operands)
    moved += sum(o.size * o.dtype.itemsize for o in out_shapes)
    vmem = pl.BlockSpec(memory_space=pltpu.VMEM)
    smem = pl.BlockSpec(memory_space=pltpu.SMEM)
    return pl.pallas_call(
        kernel,
        out_shape=out_shapes,
        in_specs=[smem] * scalars + [vmem] * (len(operands) - scalars),
        out_specs=[vmem] * len(out_shapes),
        compiler_params=pltpu.CompilerParams(vmem_limit_bytes=VMEM_LIMIT),
        cost_estimate=pl.CostEstimate(flops=int(flops * scale), bytes_accessed=int(moved * scale), transcendentals=0),
    )(*operands)


def shaped(count, shape, dtype=BF16):
    return [jax.ShapeDtypeStruct(shape, dtype) for _ in range(count)]


def tiles(width):
    return [(start, min(TILE, width - start)) for start in range(0, width, TILE)]


def split3(value):
    high = value.astype(BF16)
    rest = value - high.astype(F32)
    middle = rest.astype(BF16)
    low = (rest - middle.astype(F32)).astype(BF16)
    return high, middle, low


def tag_kernel(experts, x_hbm, ids_hbm, weights_hbm, first_ref, second_ref, ids_in, weights_in, ids_ref, weights_ref, sems):
    rows, width = x_hbm.shape
    top = ids_hbm.shape[0]
    tag_lanes = (first_ref.shape[1] + second_ref.shape[1] - width) // 2
    split = first_ref.shape[1] - tag_lanes
    ids_ref[...] = jnp.full(ids_ref.shape, -1, jnp.int32)
    weights_ref[...] = jnp.zeros(weights_ref.shape, F32)
    small = [
        pltpu.make_async_copy(ids_hbm, ids_in, sems.at[0]),
        pltpu.make_async_copy(weights_hbm, weights_in, sems.at[1]),
    ]
    large = [
        pltpu.make_async_copy(x_hbm.at[:, :split], first_ref.at[:, :split], sems.at[2]),
        pltpu.make_async_copy(x_hbm.at[:, split:], second_ref.at[:, : width - split], sems.at[3]),
    ]
    for copy in small + large:
        copy.start()
    for copy in small:
        copy.wait()
    ids_ref[:, :rows] = ids_in[...]
    weights_ref[:, :rows] = weights_in[...]
    lanes = ids_ref.shape[1]
    row = lax.broadcasted_iota(jnp.int32, (tag_lanes, lanes), 0)
    expert = row % experts
    group = row // experts
    flags = jnp.zeros((tag_lanes, lanes), F32)
    weights = jnp.zeros((tag_lanes, lanes), F32)
    for k in range(top):
        match = ids_ref[k : k + 1, :] == expert
        flags = jnp.where(match, 1.0, flags)
        weights = jnp.where(match, weights_ref[k : k + 1, :], weights)
    parts = [flags] + [part.astype(F32) for part in split3(weights)]
    tag = jnp.zeros((tag_lanes, lanes), F32)
    for number, part in enumerate(parts):
        tag = jnp.where(group == number, part, tag)
    tag = tag.T[:rows].astype(BF16)
    first_ref[:, split:] = tag
    second_ref[:, width - split :] = tag
    for copy in large:
        copy.wait()


def tagged_parts(experts, split, moe_input, route_ids, route_weights):
    rows, width = moe_input.shape
    top = route_ids.shape[1]
    tag_lanes = pl.cdiv(4 * experts, LANES) * LANES
    lanes = pl.cdiv(rows, LANES) * LANES
    return pl.pallas_call(
        functools.partial(tag_kernel, experts),
        out_shape=shaped(1, (rows, split + tag_lanes)) + shaped(1, (rows, width - split + tag_lanes)),
        in_specs=[pl.BlockSpec(memory_space=pl.ANY)] * 3,
        out_specs=[pl.BlockSpec(memory_space=pltpu.VMEM)] * 2,
        scratch_shapes=[
            pltpu.VMEM((top, rows), jnp.int32),
            pltpu.VMEM((top, rows), F32),
            pltpu.VMEM((top, lanes), jnp.int32),
            pltpu.VMEM((top, lanes), F32),
            pltpu.SemaphoreType.DMA((4,)),
        ],
        compiler_params=pltpu.CompilerParams(vmem_limit_bytes=HEAD_LIMIT),
        cost_estimate=pl.CostEstimate(flops=0, bytes_accessed=4 * rows * width, transcendentals=0),
    )(moe_input, route_ids.T, route_weights.T)


def pick_kernel(experts, cap, sources, targets, e_ref, *refs):
    x_refs, outs = refs[:sources], refs[sources : sources + targets]
    high_ref, middle_ref, low_ref = refs[sources + targets :]
    rows = x_refs[0].shape[0]
    width = outs[0].shape[1]
    total = sources * rows
    slots = sources * cap
    tag = jnp.concatenate([x[:, width:] for x in x_refs], axis=0)
    tag_lanes = tag.shape[1]
    row = lax.broadcasted_iota(jnp.int32, (total, total), 0)
    col = lax.broadcasted_iota(jnp.int32, (total, total), 1)
    before = ((row // rows == col // rows) & (col < row)).astype(F32).astype(BF16)
    rank = jnp.dot(before, tag, preferred_element_type=F32)
    tag = tag.astype(F32)
    lane = lax.broadcasted_iota(jnp.int32, (total, tag_lanes), 1)
    source = lax.broadcasted_iota(jnp.int32, (total, 1), 0) // rows
    slot = lax.broadcasted_iota(jnp.int32, (total, targets * slots), 1)
    picked = jnp.zeros((total, targets * slots), F32)
    weight = jnp.zeros((total, targets * slots), F32)
    for t in range(targets):
        e = e_ref[0, t]
        here = lane == e
        flag = jnp.sum(jnp.where(here, tag, 0.0), axis=1, keepdims=True)
        place = jnp.sum(jnp.where(here, rank, 0.0), axis=1, keepdims=True).astype(jnp.int32)
        parts = (lane % experts == e) & (lane // experts >= 1) & (lane // experts <= 3)
        factor = jnp.sum(jnp.where(parts, tag, 0.0), axis=1, keepdims=True)
        hit = slot == jnp.where(flag > 0.0, t * slots + source * cap + place, -1)
        picked = jnp.where(hit, 1.0, picked)
        weight = jnp.where(hit, factor, weight)
    high_ref[...], middle_ref[...], low_ref[...] = split3(weight)
    picker = picked.T.astype(BF16)
    for start, size in tiles(width):
        columns = pl.ds(start, size)
        x = jnp.concatenate([x[:, columns] for x in x_refs], axis=0)
        out = jnp.dot(picker, x, preferred_element_type=F32).astype(BF16)
        for t in range(targets):
            outs[t][:, columns] = out[t * slots : (t + 1) * slots]


def combine_kernel(sources, targets, *refs):
    returned = refs[:targets]
    high_ref, middle_ref, low_ref = refs[targets : targets + 3]
    outs = refs[targets + 3 :]
    rows, width = outs[0].shape
    for start, size in tiles(width):
        columns = pl.ds(start, size)
        y = jnp.concatenate([r[:, columns] for r in returned], axis=0)
        total = jnp.dot(low_ref[...], y, preferred_element_type=F32)
        total += jnp.dot(middle_ref[...], y, preferred_element_type=F32)
        total += jnp.dot(high_ref[...], y, preferred_element_type=F32)
        for s in range(sources):
            outs[s][:, columns] = total[s * rows : (s + 1) * rows].astype(outs[s].dtype)


def final_kernel(*refs):
    terms, out_ref = refs[:-1], refs[-1]
    start = 0
    while terms:
        size = terms[0].shape[1]
        count = sum(r.shape[1] == size for r in terms)
        total = terms[0][...]
        for r in terms[1:count]:
            total = total + r[...].astype(F32)
        out_ref[:, pl.ds(start, size)] = total.astype(BF16)
        terms, start = terms[count:], start + size


def reorder(blocks, planes, cap, inverse=False):
    count = blocks * planes * cap
    row = lax.broadcasted_iota(jnp.int32, (count, count), 1 if inverse else 0)
    col = lax.broadcasted_iota(jnp.int32, (count, count), 0 if inverse else 1)
    plane, block, place = row // (blocks * cap), row // cap % blocks, row % cap
    return (col == (block * planes + plane) * cap + place).astype(F32).astype(BF16)


def hidden_kernel(blocks, planes, cap, *refs):
    firsts, seconds = refs[: planes * GROUPS], refs[planes * GROUPS : planes * GROUPS + blocks]
    gate_ref, up_ref, hidden_ref = refs[planes * GROUPS + blocks :]
    split = firsts[0].shape[1]
    first = jnp.concatenate([r[...] for r in firsts], axis=0)
    second = jnp.concatenate([r[...] for r in seconds], axis=0)
    second = jnp.dot(reorder(blocks, planes, cap), second, preferred_element_type=F32).astype(BF16)

    def product(ref, columns):
        value = jnp.dot(first, ref[0, :split, columns], preferred_element_type=F32)
        return value + jnp.dot(second, ref[0, split:, columns], preferred_element_type=F32)

    for start in range(0, hidden_ref.shape[1], 256):
        columns = pl.ds(start, 256)
        gate_value = product(gate_ref, columns)
        up_value = product(up_ref, columns)
        hidden_ref[:, columns] = (gate_value * jax.nn.sigmoid(gate_value) * up_value).astype(BF16)


def chunks(split, width):
    cuts = list(range(0, split, CHUNK)) + list(range(split, width, CHUNK)) + [width]
    return [(start, stop - start) for start, stop in zip(cuts[:-1], cuts[1:])]


def load_hidden_kernel(blocks, planes, cap, *refs):
    firsts, seconds = refs[: planes * GROUPS], refs[planes * GROUPS : planes * GROUPS + blocks]
    gate_hbm, up_hbm, down_hbm, hidden_ref, gate_ref, up_ref, down_ref, gate_sum, up_sum, sems = refs[planes * GROUPS + blocks :]
    split = firsts[0].shape[1]
    pieces = chunks(split, gate_ref.shape[1])
    copies = []
    for number, (start, size) in enumerate(pieces):
        depth = pl.ds(start, size)
        copies.append((
            pltpu.make_async_copy(gate_hbm.at[:, depth], gate_ref.at[:, depth], sems.at[0, number]),
            pltpu.make_async_copy(up_hbm.at[:, depth], up_ref.at[:, depth], sems.at[1, number]),
        ))
    last = pltpu.make_async_copy(down_hbm, down_ref, sems.at[0, len(pieces)])
    for pair in copies:
        pair[0].start()
        pair[1].start()
    last.start()
    first = jnp.concatenate([r[...] for r in firsts], axis=0)
    second = jnp.concatenate([r[...] for r in seconds], axis=0)
    second = jnp.dot(reorder(blocks, planes, cap), second, preferred_element_type=F32).astype(BF16)
    for number, (start, size) in enumerate(pieces):
        x = first[:, start : start + size] if start < split else second[:, start - split : start - split + size]
        depth = pl.ds(start, size)
        for copy, ref, total in zip(copies[number], (gate_ref, up_ref), (gate_sum, up_sum)):
            copy.wait()
            part = jnp.dot(x, ref[0, depth, :], preferred_element_type=F32)
            if number == 0:
                total[...] = part
            else:
                total[...] += part
    gate_value = gate_sum[...]
    hidden_ref[...] = (gate_value * jax.nn.sigmoid(gate_value) * up_sum[...]).astype(BF16)
    last.wait()


def load_hidden(sizes, first, second, *weights):
    slots = sizes[0] * sizes[1] * sizes[2]
    split = first[0].shape[1]
    width, hidden_width = weights[0].shape[1:]
    vmem = pl.BlockSpec(memory_space=pltpu.VMEM)
    return pl.pallas_call(
        functools.partial(load_hidden_kernel, *sizes),
        out_shape=shaped(1, (slots, hidden_width)) + [jax.ShapeDtypeStruct(w.shape, w.dtype) for w in weights],
        in_specs=[vmem] * (len(first) + len(second)) + [pl.BlockSpec(memory_space=pl.ANY)] * 3,
        out_specs=[vmem] * 4,
        scratch_shapes=[
            pltpu.VMEM((slots, hidden_width), F32),
            pltpu.VMEM((slots, hidden_width), F32),
            pltpu.SemaphoreType.DMA((2, len(chunks(split, width)) + 1)),
        ],
        compiler_params=pltpu.CompilerParams(vmem_limit_bytes=LOAD_LIMIT),
        cost_estimate=pl.CostEstimate(
            flops=4 * slots * width * hidden_width,
            bytes_accessed=sum(w.size * w.dtype.itemsize for w in weights),
            transcendentals=0,
        ),
    )(*first, *second, *weights)


def down_kernel(blocks, planes, cap, hidden_ref, down_ref, first_ref, second_ref):
    split = first_ref.shape[1]
    hidden = hidden_ref[...]
    for start, size in tiles(split):
        part = jnp.dot(hidden, down_ref[0, :, pl.ds(start, size)], preferred_element_type=F32)
        first_ref[:, pl.ds(start, size)] = part.astype(BF16)
    hidden = jnp.dot(reorder(blocks, planes, cap, True), hidden, preferred_element_type=F32).astype(BF16)
    for start, size in tiles(second_ref.shape[1]):
        part = jnp.dot(hidden, down_ref[0, :, pl.ds(split + start, size)], preferred_element_type=F32)
        second_ref[:, pl.ds(start, size)] = part.astype(BF16)


def add_down_kernel(blocks, planes, cap, hidden_ref, down_ref, first_ref, second_ref, *outs):
    split = first_ref.shape[1]
    hidden = hidden_ref[...]

    def halves(hidden, base, other_ref, outs):
        rows = outs[0].shape[0]
        for start, size in tiles(other_ref.shape[1]):
            columns = pl.ds(start, size)
            part = jnp.dot(hidden, down_ref[0, :, pl.ds(base + start, size)], preferred_element_type=F32)
            both = (part + other_ref[:, columns].astype(F32)).astype(BF16)
            for number, out in enumerate(outs):
                out[:, columns] = both[number * rows : (number + 1) * rows]

    halves(hidden, 0, first_ref, outs[: planes * GROUPS])
    hidden = jnp.dot(reorder(blocks, planes, cap, True), hidden, preferred_element_type=F32).astype(BF16)
    halves(hidden, split, second_ref, outs[planes * GROUPS :])


def body(moe_input, route_ids, route_weights, gate_weight, up_weight, down_weight):
    rows, width = moe_input.shape
    top = route_ids.shape[1]
    devices = lax.axis_size("ep")
    experts = devices // 2
    cap = max(4, 2 * rows * top // devices)
    planes = min(4, experts)
    blocks = experts // planes
    slots = blocks * planes * cap
    split = width * SHARE[0] // (SHARE[1] * LANES) * LANES
    rest = width - split

    me = lax.axis_index("ep")
    my_block, my_plane = me // (2 * planes), me // 2 % planes

    def swap(array, mask):
        return lax.ppermute(array, "ep", [(i, i ^ mask) for i in range(devices)])

    def over_blocks(arrays):
        return [arrays[0]] + [swap(arrays[k], 2 * planes * k) for k in range(1, blocks)]

    def over_planes(arrays):
        return [arrays[0]] + [swap(arrays[j], 2 * j) for j in range(1, planes)]

    tagged_first, tagged_second = tagged_parts(experts, split, moe_input, route_ids, route_weights)
    plane_ids = my_block * planes + (my_plane ^ jnp.arange(planes, dtype=jnp.int32))
    block_ids = (my_block ^ jnp.arange(blocks, dtype=jnp.int32)) * planes + my_plane
    column = over_blocks([tagged_first] * blocks)
    plane = over_planes([tagged_second] * planes)
    group = blocks // GROUPS

    def pick(arrays, targets, ids, columns, scale):
        sources = len(arrays)
        out = call(
            functools.partial(pick_kernel, experts, cap, sources, targets),
            shaped(targets, (sources * cap, columns)) + shaped(3, (sources * rows, targets * sources * cap)),
            ids.reshape(1, targets), *arrays,
            flops=2 * targets * sources * cap * sources * rows * columns, scalars=1, scale=scale,
        )
        return out[:targets], out[targets:]

    first, first_factors = [], []
    for g in range(GROUPS):
        pieces, factors = pick(column[g * group : (g + 1) * group], planes, plane_ids, split, 1)
        first.append(over_planes(pieces))
        first_factors.append(factors)
    second, second_factors = pick(plane, blocks, block_ids, rest, 0.01)
    second = over_blocks(second)
    first = [first[g][j] for j in range(planes) for g in range(GROUPS)]
    first_other = [swap(piece, 1) for piece in first]
    second_other = [swap(piece, 1) for piece in second]

    sizes = (blocks, planes, cap)
    hidden_width = gate_weight.shape[2]

    def hidden_of(first, second):
        return call(
            functools.partial(hidden_kernel, *sizes),
            shaped(1, (slots, hidden_width)),
            *first, *second, gate_weight, up_weight,
            flops=4 * slots * width * hidden_width, scale=1,
        )[0]

    hidden_other, gate_weight, up_weight, down_weight = load_hidden(
        sizes, first_other, second_other, gate_weight, up_weight, down_weight
    )
    hidden_mine = hidden_of(first, second)
    parts = call(
        functools.partial(down_kernel, *sizes),
        shaped(1, (slots, split)) + shaped(1, (slots, rest)),
        hidden_other, down_weight,
        flops=2 * slots * width * hidden_width, scale=1,
    )
    results = call(
        functools.partial(add_down_kernel, *sizes),
        shaped(planes * GROUPS, (group * cap, split)) + shaped(blocks, (planes * cap, rest)),
        hidden_mine, down_weight, swap(parts[0], 1), swap(parts[1], 1),
        flops=2 * slots * width * hidden_width, scale=1,
    )
    def combine(arrays, factors, sources, columns, own, scale):
        return call(
            functools.partial(combine_kernel, sources, len(arrays)),
            shaped(own, (rows, columns), F32) + shaped(sources - own, (rows, columns)),
            *arrays, *factors,
            flops=6 * arrays[0].shape[0] * len(arrays) * sources * rows * columns,
            scale=scale,
        )

    first = []
    for g in reversed(range(GROUPS)):
        returned = over_planes(results[g : planes * GROUPS : GROUPS])
        first = list(combine(returned, first_factors[g], group, split, int(g == 0), 0.01)) + first
    first = over_blocks(first)
    second = over_blocks(results[planes * GROUPS :])
    second = over_planes(combine(second, second_factors, planes, rest, 1, 10))
    return call(final_kernel, shaped(1, (rows, width)), *first, *second, scale=1)[0]


def solution(mesh):
    return jax.shard_map(
        body,
        mesh=mesh,
        in_specs=(
            P(("groups", "ep"), None),
            P(("groups", "ep"), None),
            P(("groups", "ep"), None),
            P("ep", None, None),
            P("ep", None, None),
            P("ep", None, None),
        ),
        out_specs=P(("groups", "ep"), None),
        check_vma=False,
    )
```

```python
import functools

import jax
import jax.numpy as jnp
from jax import lax
from jax.experimental import pallas as pl
from jax.experimental.pallas import tpu as pltpu
from jax.sharding import PartitionSpec as P

F32, BF16 = jnp.float32, jnp.bfloat16
LANES = 128
SHARE = (2, 3)
TILE = 512
CHUNK = 768
VMEM_LIMIT = 24 << 20
LOAD_LIMIT = 41 << 20
HEAD_LIMIT = 24 << 20
GROUPS = 1


def call(kernel, out_shapes, *operands, flops=0, scalars=0, scale=1.0):
    moved = sum(o.size * o.dtype.itemsize for o in operands)
    moved += sum(o.size * o.dtype.itemsize for o in out_shapes)
    vmem = pl.BlockSpec(memory_space=pltpu.VMEM)
    smem = pl.BlockSpec(memory_space=pltpu.SMEM)
    return pl.pallas_call(
        kernel,
        out_shape=out_shapes,
        in_specs=[smem] * scalars + [vmem] * (len(operands) - scalars),
        out_specs=[vmem] * len(out_shapes),
        compiler_params=pltpu.CompilerParams(vmem_limit_bytes=VMEM_LIMIT),
        cost_estimate=pl.CostEstimate(flops=int(flops * scale), bytes_accessed=int(moved * scale), transcendentals=0),
    )(*operands)


def shaped(count, shape, dtype=BF16):
    return [jax.ShapeDtypeStruct(shape, dtype) for _ in range(count)]


def tiles(width):
    return [(start, min(TILE, width - start)) for start in range(0, width, TILE)]


def split3(value):
    high = value.astype(BF16)
    rest = value - high.astype(F32)
    middle = rest.astype(BF16)
    low = (rest - middle.astype(F32)).astype(BF16)
    return high, middle, low


def tag_kernel(experts, x_hbm, ids_hbm, weights_hbm, first_ref, second_ref, ids_in, weights_in, ids_ref, weights_ref, sems):
    rows, width = x_hbm.shape
    top = ids_hbm.shape[0]
    tag_lanes = (first_ref.shape[1] + second_ref.shape[1] - width) // 2
    split = first_ref.shape[1] - tag_lanes
    ids_ref[...] = jnp.full(ids_ref.shape, -1, jnp.int32)
    weights_ref[...] = jnp.zeros(weights_ref.shape, F32)
    small = [
        pltpu.make_async_copy(ids_hbm, ids_in, sems.at[0]),
        pltpu.make_async_copy(weights_hbm, weights_in, sems.at[1]),
    ]
    large = [
        pltpu.make_async_copy(x_hbm.at[:, :split], first_ref.at[:, :split], sems.at[2]),
        pltpu.make_async_copy(x_hbm.at[:, split:], second_ref.at[:, : width - split], sems.at[3]),
    ]
    for copy in small + large:
        copy.start()
    for copy in small:
        copy.wait()
    ids_ref[:, :rows] = ids_in[...]
    weights_ref[:, :rows] = weights_in[...]
    lanes = ids_ref.shape[1]
    row = lax.broadcasted_iota(jnp.int32, (tag_lanes, lanes), 0)
    expert = row % experts
    group = row // experts
    flags = jnp.zeros((tag_lanes, lanes), F32)
    weights = jnp.zeros((tag_lanes, lanes), F32)
    for k in range(top):
        match = ids_ref[k : k + 1, :] == expert
        flags = jnp.where(match, 1.0, flags)
        weights = jnp.where(match, weights_ref[k : k + 1, :], weights)
    parts = [flags] + [part.astype(F32) for part in split3(weights)]
    tag = jnp.zeros((tag_lanes, lanes), F32)
    for number, part in enumerate(parts):
        tag = jnp.where(group == number, part, tag)
    tag = tag.T[:rows].astype(BF16)
    first_ref[:, split:] = tag
    second_ref[:, width - split :] = tag
    for copy in large:
        copy.wait()


def tagged_parts(experts, split, moe_input, route_ids, route_weights):
    rows, width = moe_input.shape
    top = route_ids.shape[1]
    tag_lanes = pl.cdiv(4 * experts, LANES) * LANES
    lanes = pl.cdiv(rows, LANES) * LANES
    return pl.pallas_call(
        functools.partial(tag_kernel, experts),
        out_shape=shaped(1, (rows, split + tag_lanes)) + shaped(1, (rows, width - split + tag_lanes)),
        in_specs=[pl.BlockSpec(memory_space=pl.ANY)] * 3,
        out_specs=[pl.BlockSpec(memory_space=pltpu.VMEM)] * 2,
        scratch_shapes=[
            pltpu.VMEM((top, rows), jnp.int32),
            pltpu.VMEM((top, rows), F32),
            pltpu.VMEM((top, lanes), jnp.int32),
            pltpu.VMEM((top, lanes), F32),
            pltpu.SemaphoreType.DMA((4,)),
        ],
        compiler_params=pltpu.CompilerParams(vmem_limit_bytes=HEAD_LIMIT),
        cost_estimate=pl.CostEstimate(flops=0, bytes_accessed=4 * rows * width, transcendentals=0),
    )(moe_input, route_ids.T, route_weights.T)


def pick_kernel(experts, cap, sources, targets, e_ref, *refs):
    x_refs, outs = refs[:sources], refs[sources : sources + targets]
    high_ref, middle_ref, low_ref = refs[sources + targets :]
    rows = x_refs[0].shape[0]
    width = outs[0].shape[1]
    total = sources * rows
    slots = sources * cap
    tag = jnp.concatenate([x[:, width:] for x in x_refs], axis=0)
    tag_lanes = tag.shape[1]
    row = lax.broadcasted_iota(jnp.int32, (total, total), 0)
    col = lax.broadcasted_iota(jnp.int32, (total, total), 1)
    before = ((row // rows == col // rows) & (col < row)).astype(F32).astype(BF16)
    rank = jnp.dot(before, tag, preferred_element_type=F32)
    tag = tag.astype(F32)
    lane = lax.broadcasted_iota(jnp.int32, (total, tag_lanes), 1)
    source = lax.broadcasted_iota(jnp.int32, (total, 1), 0) // rows
    slot = lax.broadcasted_iota(jnp.int32, (total, targets * slots), 1)
    picked = jnp.zeros((total, targets * slots), F32)
    weight = jnp.zeros((total, targets * slots), F32)
    for t in range(targets):
        e = e_ref[0, t]
        here = lane == e
        flag = jnp.sum(jnp.where(here, tag, 0.0), axis=1, keepdims=True)
        place = jnp.sum(jnp.where(here, rank, 0.0), axis=1, keepdims=True).astype(jnp.int32)
        parts = (lane % experts == e) & (lane // experts >= 1) & (lane // experts <= 3)
        factor = jnp.sum(jnp.where(parts, tag, 0.0), axis=1, keepdims=True)
        hit = slot == jnp.where(flag > 0.0, t * slots + source * cap + place, -1)
        picked = jnp.where(hit, 1.0, picked)
        weight = jnp.where(hit, factor, weight)
    high_ref[...], middle_ref[...], low_ref[...] = split3(weight)
    picker = picked.T.astype(BF16)
    for start, size in tiles(width):
        columns = pl.ds(start, size)
        x = jnp.concatenate([x[:, columns] for x in x_refs], axis=0)
        out = jnp.dot(picker, x, preferred_element_type=F32).astype(BF16)
        for t in range(targets):
            outs[t][:, columns] = out[t * slots : (t + 1) * slots]


def combine_kernel(sources, targets, *refs):
    returned = refs[:targets]
    high_ref, middle_ref, low_ref = refs[targets : targets + 3]
    outs = refs[targets + 3 :]
    rows, width = outs[0].shape
    for start, size in tiles(width):
        columns = pl.ds(start, size)
        y = jnp.concatenate([r[:, columns] for r in returned], axis=0)
        total = jnp.dot(low_ref[...], y, preferred_element_type=F32)
        total += jnp.dot(middle_ref[...], y, preferred_element_type=F32)
        total += jnp.dot(high_ref[...], y, preferred_element_type=F32)
        for s in range(sources):
            outs[s][:, columns] = total[s * rows : (s + 1) * rows].astype(outs[s].dtype)


def final_kernel(*refs):
    terms, out_ref = refs[:-1], refs[-1]
    start = 0
    while terms:
        size = terms[0].shape[1]
        count = sum(r.shape[1] == size for r in terms)
        total = terms[0][...]
        for r in terms[1:count]:
            total = total + r[...].astype(F32)
        out_ref[:, pl.ds(start, size)] = total.astype(BF16)
        terms, start = terms[count:], start + size


def reorder(blocks, planes, cap, inverse=False):
    count = blocks * planes * cap
    row = lax.broadcasted_iota(jnp.int32, (count, count), 1 if inverse else 0)
    col = lax.broadcasted_iota(jnp.int32, (count, count), 0 if inverse else 1)
    plane, block, place = row // (blocks * cap), row // cap % blocks, row % cap
    return (col == (block * planes + plane) * cap + place).astype(F32).astype(BF16)


def hidden_kernel(blocks, planes, cap, *refs):
    firsts, seconds = refs[: planes * GROUPS], refs[planes * GROUPS : planes * GROUPS + blocks]
    gate_ref, up_ref, hidden_ref = refs[planes * GROUPS + blocks :]
    split = firsts[0].shape[1]
    first = jnp.concatenate([r[...] for r in firsts], axis=0)
    second = jnp.concatenate([r[...] for r in seconds], axis=0)
    second = jnp.dot(reorder(blocks, planes, cap), second, preferred_element_type=F32).astype(BF16)

    def product(ref, columns):
        value = jnp.dot(first, ref[0, :split, columns], preferred_element_type=F32)
        return value + jnp.dot(second, ref[0, split:, columns], preferred_element_type=F32)

    for start in range(0, hidden_ref.shape[1], 256):
        columns = pl.ds(start, 256)
        gate_value = product(gate_ref, columns)
        up_value = product(up_ref, columns)
        hidden_ref[:, columns] = (gate_value * jax.nn.sigmoid(gate_value) * up_value).astype(BF16)


def chunks(split, width):
    cuts = list(range(0, split, CHUNK)) + list(range(split, width, CHUNK)) + [width]
    return [(start, stop - start) for start, stop in zip(cuts[:-1], cuts[1:])]


def load_hidden_kernel(blocks, planes, cap, *refs):
    firsts, seconds = refs[: planes * GROUPS], refs[planes * GROUPS : planes * GROUPS + blocks]
    gate_hbm, up_hbm, down_hbm, hidden_ref, gate_ref, up_ref, down_ref, gate_sum, up_sum, sems = refs[planes * GROUPS + blocks :]
    split = firsts[0].shape[1]
    pieces = chunks(split, gate_ref.shape[1])
    copies = []
    for number, (start, size) in enumerate(pieces):
        depth = pl.ds(start, size)
        copies.append((
            pltpu.make_async_copy(gate_hbm.at[:, depth], gate_ref.at[:, depth], sems.at[0, number]),
            pltpu.make_async_copy(up_hbm.at[:, depth], up_ref.at[:, depth], sems.at[1, number]),
        ))
    last = pltpu.make_async_copy(down_hbm, down_ref, sems.at[0, len(pieces)])
    for pair in copies:
        pair[0].start()
        pair[1].start()
    last.start()
    first = jnp.concatenate([r[...] for r in firsts], axis=0)
    second = jnp.concatenate([r[...] for r in seconds], axis=0)
    second = jnp.dot(reorder(blocks, planes, cap), second, preferred_element_type=F32).astype(BF16)
    for number, (start, size) in enumerate(pieces):
        x = first[:, start : start + size] if start < split else second[:, start - split : start - split + size]
        depth = pl.ds(start, size)
        for copy, ref, total in zip(copies[number], (gate_ref, up_ref), (gate_sum, up_sum)):
            copy.wait()
            part = jnp.dot(x, ref[0, depth, :], preferred_element_type=F32)
            if number == 0:
                total[...] = part
            else:
                total[...] += part
    gate_value = gate_sum[...]
    hidden_ref[...] = (gate_value * jax.nn.sigmoid(gate_value) * up_sum[...]).astype(BF16)
    last.wait()


def load_hidden(sizes, first, second, *weights):
    slots = sizes[0] * sizes[1] * sizes[2]
    split = first[0].shape[1]
    width, hidden_width = weights[0].shape[1:]
    vmem = pl.BlockSpec(memory_space=pltpu.VMEM)
    return pl.pallas_call(
        functools.partial(load_hidden_kernel, *sizes),
        out_shape=shaped(1, (slots, hidden_width)) + [jax.ShapeDtypeStruct(w.shape, w.dtype) for w in weights],
        in_specs=[vmem] * (len(first) + len(second)) + [pl.BlockSpec(memory_space=pl.ANY)] * 3,
        out_specs=[vmem] * 4,
        scratch_shapes=[
            pltpu.VMEM((slots, hidden_width), F32),
            pltpu.VMEM((slots, hidden_width), F32),
            pltpu.SemaphoreType.DMA((2, len(chunks(split, width)) + 1)),
        ],
        compiler_params=pltpu.CompilerParams(vmem_limit_bytes=LOAD_LIMIT),
        cost_estimate=pl.CostEstimate(
            flops=4 * slots * width * hidden_width,
            bytes_accessed=sum(w.size * w.dtype.itemsize for w in weights),
            transcendentals=0,
        ),
    )(*first, *second, *weights)


def down_kernel(sizes, base, reordered, added, hidden_ref, down_ref, *refs):
    hidden = hidden_ref[...]
    if reordered:
        hidden = jnp.dot(reorder(*sizes, True), hidden, preferred_element_type=F32).astype(BF16)
    outs = refs[1:] if added else refs
    rows = outs[0].shape[0]
    for start, size in tiles(outs[0].shape[1]):
        columns = pl.ds(start, size)
        part = jnp.dot(hidden, down_ref[0, :, pl.ds(base + start, size)], preferred_element_type=F32)
        if added:
            part += refs[0][:, columns].astype(F32)
        part = part.astype(BF16)
        for number, out in enumerate(outs):
            out[:, columns] = part[number * rows : (number + 1) * rows]


def body(moe_input, route_ids, route_weights, gate_weight, up_weight, down_weight):
    rows, width = moe_input.shape
    top = route_ids.shape[1]
    devices = lax.axis_size("ep")
    experts = devices // 2
    cap = max(4, 2 * rows * top // devices)
    planes = min(4, experts)
    blocks = experts // planes
    slots = blocks * planes * cap
    split = width * SHARE[0] // (SHARE[1] * LANES) * LANES
    rest = width - split

    me = lax.axis_index("ep")
    my_block, my_plane = me // (2 * planes), me // 2 % planes

    def swap(array, mask):
        return lax.ppermute(array, "ep", [(i, i ^ mask) for i in range(devices)])

    def over_blocks(arrays):
        return [arrays[0]] + [swap(arrays[k], 2 * planes * k) for k in range(1, blocks)]

    def over_planes(arrays):
        return [arrays[0]] + [swap(arrays[j], 2 * j) for j in range(1, planes)]

    tagged_first, tagged_second = tagged_parts(experts, split, moe_input, route_ids, route_weights)
    plane_ids = my_block * planes + (my_plane ^ jnp.arange(planes, dtype=jnp.int32))
    block_ids = (my_block ^ jnp.arange(blocks, dtype=jnp.int32)) * planes + my_plane
    column = over_blocks([tagged_first] * blocks)
    plane = over_planes([tagged_second] * planes)
    group = blocks // GROUPS

    def pick(arrays, targets, ids, columns, scale):
        sources = len(arrays)
        out = call(
            functools.partial(pick_kernel, experts, cap, sources, targets),
            shaped(targets, (sources * cap, columns)) + shaped(3, (sources * rows, targets * sources * cap)),
            ids.reshape(1, targets), *arrays,
            flops=2 * targets * sources * cap * sources * rows * columns, scalars=1, scale=scale,
        )
        return out[:targets], out[targets:]

    first, first_factors = [], []
    for g in range(GROUPS):
        pieces, factors = pick(column[g * group : (g + 1) * group], planes, plane_ids, split, 1)
        first.append(over_planes(pieces))
        first_factors.append(factors)
    second, second_factors = pick(plane, blocks, block_ids, rest, 0.01)
    second = over_blocks(second)
    first = [first[g][j] for j in range(planes) for g in range(GROUPS)]
    first_other = [swap(piece, 1) for piece in first]
    second_other = [swap(piece, 1) for piece in second]

    sizes = (blocks, planes, cap)
    hidden_width = gate_weight.shape[2]

    def hidden_of(first, second):
        return call(
            functools.partial(hidden_kernel, *sizes),
            shaped(1, (slots, hidden_width)),
            *first, *second, gate_weight, up_weight,
            flops=4 * slots * width * hidden_width, scale=1,
        )[0]

    hidden_other, gate_weight, up_weight, down_weight = load_hidden(
        sizes, first_other, second_other, gate_weight, up_weight, down_weight
    )
    hidden_mine = hidden_of(first, second)
    def down(hidden, base, count, columns, *received):
        return call(
            functools.partial(down_kernel, sizes, base, base > 0, len(received) > 0),
            shaped(count, (slots // count, columns)),
            hidden, down_weight, *received,
            flops=2 * slots * columns * hidden_width,
        )

    other_second = swap(down(hidden_other, split, 1, rest)[0], 1)
    other_first = swap(down(hidden_other, 0, 1, split)[0], 1)
    results_second = down(hidden_mine, split, blocks, rest, other_second)
    results_first = down(hidden_mine, 0, planes, split, other_first)
    results = list(results_first) + list(results_second)

    def combine(arrays, factors, sources, columns, own, scale):
        return call(
            functools.partial(combine_kernel, sources, len(arrays)),
            shaped(own, (rows, columns), F32) + shaped(sources - own, (rows, columns)),
            *arrays, *factors,
            flops=6 * arrays[0].shape[0] * len(arrays) * sources * rows * columns,
            scale=scale,
        )

    first = []
    for g in reversed(range(GROUPS)):
        returned = over_planes(results[g : planes * GROUPS : GROUPS])
        first = list(combine(returned, first_factors[g], group, split, int(g == 0), 0.01)) + first
    first = over_blocks(first)
    second = over_blocks(results[planes * GROUPS :])
    second = over_planes(combine(second, second_factors, planes, rest, 1, 10))
    return call(final_kernel, shaped(1, (rows, width)), *first, *second, scale=1)[0]


def solution(mesh):
    return jax.shard_map(
        body,
        mesh=mesh,
        in_specs=(
            P(("groups", "ep"), None),
            P(("groups", "ep"), None),
            P(("groups", "ep"), None),
            P("ep", None, None),
            P("ep", None, None),
            P("ep", None, None),
        ),
        out_specs=P(("groups", "ep"), None),
        check_vma=False,
    )
```
